128 devices in a mesh: chan: 8 (over x_hi, y), tmpl: 16 (over z, x_lo, core).
Axes of the slice: x: 4 (x_hi: 2, x_lo: 2; x = x_hi * 2 + x_lo), y: 4, z: 4, core: 2. Of those that a mesh axis runs over, the one named last changes fastest.
Arguments:
- samples: bfloat16 [16, 2048, 1024], P(None, 'chan', 'tmpl'), may hold values from -20 to 20
- template_spectra: bfloat16 [2, 256, 2048, 512], P(None, 'tmpl', 'chan'), may hold values from -6 to 6
- lag_lengths: int32 [256], P('tmpl'), may hold values from 64 to 512
- offsets: int32 [16], replicated, may hold values from 0 to 1023
Outputs:
- stacked: float32 [256, 1024], P('tmpl', 'chan')
The draws below stay inside these ranges and needn't reach their ends.
All inputs are finite; a program needn't handle non-finite values.
Results may differ from the reference program's by a relative error of at most 0.009.
Values may be sent and summed in bfloat16 or wider, within the bound.
No kernel may reach another device: no remote copies, remote signals or barrier semaphores. Data moves between devices by JAX's collectives and lax.ppermute only.
A program may use at most 128 MiB of HBM per device.

```python
import math
import jax
import jax.numpy as jnp
from jax import lax

CH = 2048
NF = 512
NT = 1024
S = 16
TEMPLATES = 256


def draw_samples(key, part):
    key = jax.random.fold_in(key, 1)
    noise_key, level_key = jax.random.split(key, 2)
    repeats = NT // 32
    level = jax.random.uniform(level_key, (S, 1, 32), minval=-1.2, maxval=1.2)
    amplitude = jnp.repeat(jnp.exp(level), repeats, axis=2)
    noise = jax.random.truncated_normal(noise_key, -4.0, 4.0, (S, CH, NT))
    return (noise * amplitude).astype(jnp.bfloat16)


def touch_ends(values, rng, low, largest):
    dims = values.shape
    index_at = [jax.random.randint(jax.random.fold_in(rng, axis), (), 0, dims[axis]) for axis in range(len(dims))]
    values = values.at[tuple(index_at)].set(low)
    longest = dims.index(max(dims))
    index_at[longest] = (index_at[longest] + 1) % dims[longest]
    return values.at[tuple(index_at)].set(largest)


def steps_of(key, dims, pieces, smallest, high):
    level, own = 1.0, jax.random.fold_in(key, 6)
    for position, parts in pieces:
        draws = jnp.exp(jax.random.uniform(jax.random.fold_in(own, position), (parts,), jnp.float32, smallest / len(pieces), high / len(pieces)))
        level = level * jnp.repeat(draws, dims[position] // parts).reshape([-1 if axis == position else 1 for axis in range(len(dims))])
    return level


def bell_draw(own_key, shape, spread, most, shards=(), kind=jnp.bfloat16):
    level = steps_of(own_key, shape, shards, -0.22, 0.18) if shards else 1.0
    result = jax.random.normal(own_key, shape, jnp.float32) * spread * level
    return jnp.minimum(jnp.maximum(result, -most), most).astype(kind)


def setup_inputs(seed: int = 0) -> dict:
    seeds = jax.random.split(jax.random.key(seed), 5)
    samples = draw_samples(jax.random.fold_in(seeds[4], 71), 0)
    template_spectra = bell_draw(seeds[1], (2, TEMPLATES, CH, NF), 1.0, 6.0, ((1, 16), (2, 8)))
    lag_lengths = touch_ends(jax.random.randint(seeds[2], (TEMPLATES,), NT // 16, NT // 2 + 1), jax.random.fold_in(seeds[2], 1), NT // 16, (NT // 2 + 1) - 1).astype(jnp.int32)
    offsets = touch_ends(jax.random.randint(seeds[3], (S,), 0, NT), jax.random.fold_in(seeds[3], 1), 0, NT - 1).astype(jnp.int32)
    return dict(samples=samples, template_spectra=template_spectra, lag_lengths=lag_lengths, offsets=offsets)


epsilon = 1e-06
highest = lax.Precision.HIGHEST

def twiddles(length, bin_count):
    sample_index = lax.iota(jnp.int32, length)
    bin_index = lax.iota(jnp.int32, bin_count)
    phase = sample_index[:, None] * bin_index[None, :] % length
    angle = phase.astype(jnp.float32) * (2.0 * math.pi / length)
    return (jnp.cos(angle), jnp.sin(angle))

def inverse_table(bin_count):
    length = 2 * bin_count
    cosine, sine = twiddles(length, bin_count)
    return jnp.concatenate([cosine.T, -sine.T], axis=0) * (2.0 / length)

def window_powers(energy, lag_lengths, channel_total):
    length = energy.shape[1]
    doubled = jnp.concatenate([energy, energy], axis=1)
    prefix = jnp.concatenate([jnp.zeros((energy.shape[0], 1), jnp.float32), jnp.cumsum(doubled, axis=1)], axis=1)

    def single(window):
        ahead = lax.dynamic_slice_in_dim(prefix, window.astype(jnp.int32), length, 1)
        return (ahead - prefix[:, :length]) / (channel_total * window.astype(jnp.float32))
    return jax.vmap(single)(lag_lengths)

def stack_segments(scores, offsets, segment_total):

    def single(block, shift_by):
        return jnp.roll(block, shift_by, axis=1)
    rolled = jax.vmap(single, in_axes=(1, 0), out_axes=1)(scores, offsets)
    return lax.optimization_barrier(jnp.sum(rolled, axis=1)) / math.sqrt(segment_total)

def reference(samples, template_spectra, lag_lengths, offsets):
    segment_total, channel_total, length = samples.shape
    bin_count = length // 2
    wide = samples.astype(jnp.float32)
    freq = jnp.fft.rfft(wide, axis=2)[:, :, :bin_count]
    spectra = jnp.concatenate([jnp.real(freq), jnp.imag(freq)], axis=2).astype(jnp.bfloat16)
    data_real = spectra[:, :, :bin_count].astype(jnp.float32)
    data_imag = spectra[:, :, bin_count:].astype(jnp.float32)
    energy = lax.optimization_barrier(jnp.sum(wide * wide, axis=1))
    backward = inverse_table(bin_count)
    block_size = 8
    real_blocks = template_spectra[0].reshape(-1, block_size, channel_total, bin_count)
    imag_blocks = template_spectra[1].reshape(-1, block_size, channel_total, bin_count)

    def per_block(pair):
        real_tmpl = pair[0].astype(jnp.float32)
        imag_tmpl = pair[1].astype(jnp.float32)

        def product(left, right):
            return jnp.einsum('tcf,scf->tsf', left, right, precision=highest)
        real_part = product(real_tmpl, data_real) + product(imag_tmpl, data_imag)
        imag_part = product(real_tmpl, data_imag) - product(imag_tmpl, data_real)
        cross = jnp.concatenate([real_part, imag_part], axis=2)
        correlation = jnp.dot(cross, backward, precision=highest)
        tmpl_energy = lax.optimization_barrier(jnp.sum(real_tmpl * real_tmpl + imag_tmpl * imag_tmpl, axis=(1, 2))) * (2.0 / length)
        return (correlation, tmpl_energy)
    correlation, tmpl_energy = lax.map(per_block, (real_blocks, imag_blocks))
    correlation = correlation.reshape(-1, segment_total, length)
    tmpl_energy = tmpl_energy.reshape(-1)
    powers = window_powers(energy, lag_lengths, channel_total)
    scores = correlation / jnp.sqrt(tmpl_energy[:, None, None] * powers + epsilon)
    return stack_segments(scores, offsets, segment_total)
```

```python
import math

import jax
import jax.numpy as jnp
import numpy as np
from jax import lax
from jax.experimental import pallas as pl
from jax.experimental.pallas import tpu as pltpu
from jax.sharding import PartitionSpec as P

epsilon = 1e-06
LANES = 128
BLOCK = 16
F32 = jnp.float32
BF16 = jnp.bfloat16


def tables(length):
    bins = length // 2
    angle = 2.0 * np.pi * (np.outer(np.arange(bins), np.arange(length)) % length) / length
    forward = np.concatenate([np.cos(angle), -np.sin(angle)], axis=0)
    backward = forward * (2.0 / length)
    backward_high = backward.astype(BF16)
    backward_low = (backward - backward_high.astype(np.float64)).astype(BF16)
    return forward.astype(BF16), backward_high, backward_low


def selection(segments, templates):
    rows = np.arange(segments * templates * BLOCK) // BLOCK
    return (rows[:, None] == np.arange(segments * templates)[None, :]).astype(BF16)


def template_kernel(g_ref, out_ref, energy_ref):
    t = pl.program_id(0)
    channels, bins = g_ref.shape[2:]
    total = jnp.zeros((1, bins), F32)
    for part in range(2):
        wide = g_ref[part, 0].astype(F32)
        total = total + jnp.sum(wide * wide, axis=0, keepdims=True)
        flipped = wide.T.astype(BF16)
        out_ref[:, 0, :, part * channels : (part + 1) * channels] = flipped.reshape(
            bins // BLOCK, BLOCK, channels
        )
    folded = total[:, :LANES]
    for j in range(1, bins // LANES):
        folded = folded + total[:, j * LANES : (j + 1) * LANES]
    energy_ref[pl.ds(t, 1), :] = folded


def prepare_templates(template_spectra):
    _, templates, channels, bins = template_spectra.shape
    return pl.pallas_call(
        template_kernel,
        grid=(templates,),
        in_specs=[pl.BlockSpec((2, 1, channels, bins), lambda t: (0, t, 0, 0))],
        out_specs=[
            pl.BlockSpec((bins // BLOCK, 1, BLOCK, 2 * channels), lambda t: (0, t, 0, 0)),
            pl.BlockSpec((templates, LANES), lambda t: (0, 0)),
        ],
        out_shape=[
            jax.ShapeDtypeStruct((bins // BLOCK, templates, BLOCK, 2 * channels), BF16),
            jax.ShapeDtypeStruct((templates, LANES), F32),
        ],
        compiler_params=pltpu.CompilerParams(vmem_limit_bytes=24 << 20),
        cost_estimate=pl.CostEstimate(flops=20_000_000, bytes_accessed=16 << 20, transcendentals=0),
        name="template_flip",
    )(template_spectra)


def weight_kernel(channel_total, scale, lag_ref, offset_ref, level_ref, energy_ref, out_ref, prefix):
    segments, length = energy_ref.shape
    templates = out_ref.shape[1]
    row = lax.broadcasted_iota(jnp.int32, (segments, length), 0)
    energy = energy_ref[...]
    delayed = jnp.zeros((segments, length), F32)
    for s in range(segments):
        delayed = jnp.where(row == s, pltpu.roll(energy, offset_ref[s], axis=1), delayed)
    before = lax.broadcasted_iota(jnp.int32, (LANES, LANES), 0) < lax.broadcasted_iota(
        jnp.int32, (LANES, LANES), 1
    )
    before = before.astype(F32)
    carry = jnp.zeros((segments, 1), F32)
    blocks = length // LANES
    for j in range(blocks):
        piece = delayed[:, j * LANES : (j + 1) * LANES]
        prefix[:, j * LANES : (j + 1) * LANES] = carry + jnp.dot(
            piece, before, precision=lax.Precision.HIGHEST, preferred_element_type=F32
        )
        carry = carry + jnp.sum(piece, axis=1, keepdims=True)
    first = prefix[:, :length]
    prefix[:, length : 2 * length] = first + carry
    prefix[:, 2 * length :] = first[:, :LANES] + 2.0 * carry
    span = length + LANES
    for t in range(templates):
        lag = lag_ref[t]
        start = pl.multiple_of((lag // LANES) * LANES, LANES)
        ahead = pltpu.roll(prefix[:, pl.ds(start, span)], span - lag % LANES, axis=1)[:, :length]
        power = (ahead - first) / (channel_total * lag.astype(F32))
        out_ref[:, t, :] = scale * lax.rsqrt(level_ref[t] * power + epsilon)


def score_weights(lag_lengths, offsets, level, energy, channel_total):
    segments, length = energy.shape
    templates = lag_lengths.shape[0]
    smem = pl.BlockSpec(memory_space=pltpu.SMEM)
    vmem = pl.BlockSpec(memory_space=pltpu.VMEM)

    def kernel(*refs):
        weight_kernel(channel_total, 1.0 / math.sqrt(segments), *refs)

    return pl.pallas_call(
        kernel,
        in_specs=[smem, smem, smem, vmem],
        out_specs=vmem,
        out_shape=jax.ShapeDtypeStruct((segments, templates, length), F32),
        scratch_shapes=[pltpu.VMEM((segments, 2 * length + LANES), F32)],
        compiler_params=pltpu.CompilerParams(vmem_limit_bytes=16 << 20),
        cost_estimate=pl.CostEstimate(flops=20_000_000, bytes_accessed=2 << 20, transcendentals=262144),
        name="score_weights",
    )(lag_lengths, offsets, level, energy)


def detect_kernel(
    x_ref, weight_ref, cos_ref, sin_ref, forward_ref, select_ref, tmpl_hbm, high_hbm, low_hbm,
    out_ref, tmpl, high, low, spectra, masked, sems,
):
    half = pl.program_id(0)
    blocks, segments, piece, channels = x_ref.shape
    length = blocks * piece
    bins = length // 2
    templates = weight_ref.shape[1]
    lanes = templates * BLOCK
    copies = [
        pltpu.make_async_copy(tmpl_hbm, tmpl, sems.at[0]),
        pltpu.make_async_copy(high_hbm, high, sems.at[1]),
        pltpu.make_async_copy(low_hbm, low, sems.at[2]),
    ]

    @pl.when(half == 0)
    def _():
        for copy in copies:
            copy.start()

    @pl.loop(0, segments)
    def _(s):
        record = x_ref[:, pl.ds(s, 1)].reshape(length, channels)
        result = jnp.dot(forward_ref[...], record, preferred_element_type=F32)
        real = result[:bins].astype(BF16)
        imag = result[bins:].astype(BF16)
        spectra[0, s, :, :channels] = real
        spectra[0, s, :, channels:] = imag
        spectra[1, s, :, :channels] = imag
        spectra[1, s, :, channels:] = -real

    @pl.when(half == 0)
    def _():
        for copy in copies:
            copy.wait()

    rows = 2 * segments * BLOCK
    keep = (
        lax.broadcasted_iota(jnp.int32, (rows, lanes), 0) % BLOCK
        == lax.broadcasted_iota(jnp.int32, (rows, lanes), 1) % BLOCK
    )

    @pl.loop(0, bins // BLOCK)
    def _(b):
        start = pl.multiple_of(b * BLOCK, BLOCK)
        left = spectra[:, :, pl.ds(start, BLOCK), :].reshape(rows, 2 * channels)
        right = tmpl[b].reshape(lanes, 2 * channels)
        product = lax.dot_general(left, right, (((1,), (1,)), ((), ())), preferred_element_type=F32)
        product = jnp.where(keep, product, 0.0).astype(BF16)
        for part in range(2):
            for s in range(segments):
                first = (part * segments + s) * BLOCK
                masked[pl.ds(part * bins + start, BLOCK), s * lanes : (s + 1) * lanes] = product[
                    first : first + BLOCK
                ]

    cross = jnp.dot(masked[...], select_ref[...], preferred_element_type=F32)
    real, imag = cross[:bins], cross[bins:]
    cosine, sine = cos_ref[...], sin_ref[...]
    delayed = jnp.concatenate([real * cosine + imag * sine, imag * cosine - real * sine], axis=0)
    delayed_high = delayed.astype(BF16)
    delayed_low = (delayed - delayed_high.astype(F32)).astype(BF16)

    def back(left, right):
        return lax.dot_general(left, right, (((0,), (0,)), ((), ())), preferred_element_type=F32)

    correlation = back(delayed_high, high[...]) + back(delayed_low, high[...])
    correlation = correlation + back(delayed_high, low[...])
    scores = correlation.reshape(segments, templates, length) * weight_ref[...]
    stack = jnp.sum(scores, axis=0)

    @pl.when(half == 0)
    def _():
        for j in range(length // LANES):
            out_ref[j] = stack[:, j * LANES : (j + 1) * LANES]

    @pl.when(half != 0)
    def _():
        for j in range(length // LANES):
            out_ref[j] += stack[:, j * LANES : (j + 1) * LANES]


def detect(record, weights, cosine, sine, forward, high, low, tmpl, halves):
    pieces, segments, piece, channels = record.shape
    length = pieces * piece
    templates = weights.shape[1]
    step = segments // halves
    select = selection(step, templates)
    once = pl.Buffered(1)
    anywhere = pl.BlockSpec(memory_space=pl.ANY)

    def fixed(array):
        return pl.BlockSpec(array.shape, lambda h: (0,) * array.ndim, pipeline_mode=once)

    return pl.pallas_call(
        detect_kernel,
        grid=(halves,),
        in_specs=[
            pl.BlockSpec((pieces, step, piece, channels), lambda h: (0, h, 0, 0)),
            pl.BlockSpec((step, templates, length), lambda h: (h, 0, 0)),
            pl.BlockSpec((length // 2, step * templates), lambda h: (0, h)),
            pl.BlockSpec((length // 2, step * templates), lambda h: (0, h)),
            fixed(forward),
            fixed(select),
            anywhere,
            anywhere,
            anywhere,
        ],
        out_specs=pl.BlockSpec((length // LANES, templates, LANES), lambda h: (0, 0, 0)),
        out_shape=jax.ShapeDtypeStruct((length // LANES, templates, LANES), F32),
        scratch_shapes=[
            pltpu.VMEM(tmpl.shape, BF16),
            pltpu.VMEM(high.shape, BF16),
            pltpu.VMEM(low.shape, BF16),
            pltpu.VMEM((2, step, length // 2, 2 * channels), BF16),
            pltpu.VMEM((length, step * templates * BLOCK), BF16),
            pltpu.SemaphoreType.DMA((3,)),
        ],
        compiler_params=pltpu.CompilerParams(vmem_limit_bytes=56 << 20),
        cost_estimate=pl.CostEstimate(flops=30_000_000_000, bytes_accessed=32 << 20, transcendentals=0),
        name="detect",
    )(record, weights, cosine, sine, forward, select, tmpl, high, low)


def swap(value, axis, partner):
    return lax.ppermute(value, axis, [(i, partner(i)) for i in range(lax.axis_size(axis))])


def body(samples, template_spectra, lag_lengths, offsets):
    segments, channels, piece = samples.shape
    chan_groups = lax.axis_size("chan")
    tmpl_groups = lax.axis_size("tmpl")
    channel_total = channels * chan_groups
    length = piece * tmpl_groups
    bins = length // 2
    templates = template_spectra.shape[1]

    record = lax.all_gather(jnp.transpose(samples, (0, 2, 1)), "tmpl", axis=0, tiled=False)

    wide = samples.astype(F32)
    energy = jnp.sum(wide * wide, axis=1)
    tmpl, level = prepare_templates(template_spectra)
    level = jnp.sum(level, axis=1) * (2.0 / length)

    sums = jnp.concatenate([energy, level.reshape(segments, -1)], axis=1)
    for bit in (1, 2, 4):
        sums = sums + swap(sums, "chan", lambda i: i ^ bit)
    energy = sums[:, :piece]
    level = sums[:, piece:].reshape(templates)
    me = lax.axis_index("tmpl")
    for bit in (1, 2, 4, 8):
        other = swap(energy, "tmpl", lambda i: i ^ bit)
        upper = (me & bit) != 0
        energy = jnp.concatenate(
            [jnp.where(upper, other, energy), jnp.where(upper, energy, other)], axis=1
        )
    weights = score_weights(lag_lengths, offsets, level, energy, channel_total)

    phase = offsets[None, :] * lax.iota(jnp.int32, bins)[:, None] % length
    angle = phase.astype(F32) * (2.0 * math.pi / length)
    cosine = jnp.repeat(jnp.cos(angle), templates, axis=1)
    sine = jnp.repeat(jnp.sin(angle), templates, axis=1)
    forward, high, low = tables(length)
    partial = detect(record, weights, cosine, sine, forward, high, low, tmpl, 2)
    return jnp.sum(
        lax.all_to_all(partial, "chan", 0, 0, tiled=False), axis=0
    )


def solution(mesh):
    return jax.shard_map(
        body,
        mesh=mesh,
        in_specs=(P(None, "chan", "tmpl"), P(None, "tmpl", "chan", None), P("tmpl"), P()),
        out_specs=P("tmpl", "chan"),
        check_vma=False,
    )
```

```python
import math

import jax
import jax.numpy as jnp
import numpy as np
from jax import lax
from jax.experimental import pallas as pl
from jax.experimental.pallas import tpu as pltpu
from jax.sharding import PartitionSpec as P

epsilon = 1e-06
LANES = 128
BLOCK = 16
F32 = jnp.float32
BF16 = jnp.bfloat16


def bin_order(bins):
    return np.concatenate([np.arange(0, bins, 2), np.arange(1, bins, 2)])


def tables(length):
    bins = length // 2
    angle = 2.0 * np.pi * (np.outer(bin_order(bins), np.arange(length)) % length) / length
    cosine, sine = np.cos(angle), -np.sin(angle)
    near = bins // 2
    even = np.concatenate([cosine[:near, :bins], sine[:near, :bins]], axis=0)
    odd = np.concatenate([cosine[near:, :bins], sine[near:, :bins]], axis=0)
    backward = np.concatenate([cosine, sine], axis=0) * (2.0 / length)
    high = backward.astype(BF16)
    low = (backward - high.astype(np.float64)).astype(BF16)
    return even.astype(BF16), odd.astype(BF16), high, low


def template_kernel(g_ref, out_ref, energy_ref, flipped):
    t = pl.program_id(0)
    channels, bins = g_ref.shape[2:]
    total = jnp.zeros((1, bins), F32)
    for part in range(2):
        wide = g_ref[part, 0].astype(F32)
        total = total + jnp.sum(wide * wide, axis=0, keepdims=True)
        turned = wide.T
        half = bins // 2 // BLOCK
        for j in range(channels // LANES):
            flipped[j] = turned[:, j * LANES : (j + 1) * LANES]
            first = part * channels + j * LANES
            for parity in range(2):
                rows = flipped[j, pl.ds(parity, bins // 2, stride=2), :].astype(BF16)
                out_ref[parity * half : (parity + 1) * half, 0, :, first : first + LANES] = (
                    rows.reshape(half, BLOCK, LANES)
                )
    folded = total[:, :LANES]
    for j in range(1, bins // LANES):
        folded = folded + total[:, j * LANES : (j + 1) * LANES]
    energy_ref[pl.ds(t, 1), :] = folded


def prepare_templates(template_spectra):
    _, templates, channels, bins = template_spectra.shape
    return pl.pallas_call(
        template_kernel,
        grid=(templates,),
        in_specs=[pl.BlockSpec((2, 1, channels, bins), lambda t: (0, t, 0, 0))],
        out_specs=[
            pl.BlockSpec((bins // BLOCK, 1, BLOCK, 2 * channels), lambda t: (0, t, 0, 0)),
            pl.BlockSpec((templates, LANES), lambda t: (0, 0)),
        ],
        out_shape=[
            jax.ShapeDtypeStruct((bins // BLOCK, templates, BLOCK, 2 * channels), BF16),
            jax.ShapeDtypeStruct((templates, LANES), F32),
        ],
        scratch_shapes=[pltpu.VMEM((channels // LANES, bins, LANES), F32)],
        compiler_params=pltpu.CompilerParams(vmem_limit_bytes=12 << 20),
        cost_estimate=pl.CostEstimate(flops=20_000_000, bytes_accessed=16 << 20, transcendentals=0),
        name="template_flip",
    )(template_spectra)


def weight_kernel(channel_total, scale, lag_ref, offset_ref, level_ref, energy_ref, out_ref, prefix):
    segments, length = energy_ref.shape
    templates = out_ref.shape[0]
    row = lax.broadcasted_iota(jnp.int32, (segments, length), 0)
    energy = energy_ref[...]
    delayed = jnp.zeros((segments, length), F32)
    for s in range(segments):
        delayed = jnp.where(row == s, pltpu.roll(energy, offset_ref[s], axis=1), delayed)
    before = lax.broadcasted_iota(jnp.int32, (LANES, LANES), 0) < lax.broadcasted_iota(
        jnp.int32, (LANES, LANES), 1
    )
    before = before.astype(F32)
    carry = jnp.zeros((segments, 1), F32)
    blocks = length // LANES
    for j in range(blocks):
        piece = delayed[:, j * LANES : (j + 1) * LANES]
        prefix[:, j * LANES : (j + 1) * LANES] = carry + jnp.dot(
            piece, before, precision=lax.Precision.HIGHEST, preferred_element_type=F32
        )
        carry = carry + jnp.sum(piece, axis=1, keepdims=True)
    first = prefix[:, :length]
    prefix[:, length : 2 * length] = first + carry
    prefix[:, 2 * length :] = first[:, :LANES] + 2.0 * carry
    span = length + LANES
    for t in range(templates):
        lag = lag_ref[t]
        start = pl.multiple_of((lag // LANES) * LANES, LANES)
        ahead = pltpu.roll(prefix[:, pl.ds(start, span)], span - lag % LANES, axis=1)[:, :length]
        power = (ahead - first) / (channel_total * lag.astype(F32))
        out_ref[t] = scale * lax.rsqrt(level_ref[t] * power + epsilon)


def score_weights(lag_lengths, offsets, level, energy, channel_total):
    segments, length = energy.shape
    templates = lag_lengths.shape[0]
    smem = pl.BlockSpec(memory_space=pltpu.SMEM)
    vmem = pl.BlockSpec(memory_space=pltpu.VMEM)

    def kernel(*refs):
        weight_kernel(channel_total, 1.0 / math.sqrt(segments), *refs)

    return pl.pallas_call(
        kernel,
        in_specs=[smem, smem, smem, vmem],
        out_specs=vmem,
        out_shape=jax.ShapeDtypeStruct((templates, segments, length), F32),
        scratch_shapes=[pltpu.VMEM((segments, 2 * length + LANES), F32)],
        compiler_params=pltpu.CompilerParams(vmem_limit_bytes=16 << 20),
        cost_estimate=pl.CostEstimate(flops=20_000_000, bytes_accessed=2 << 20, transcendentals=262144),
        name="score_weights",
    )(lag_lengths, offsets, level, energy)


def store_spectra(spectra, s, even_ref, odd_ref, summed, differed):
    near, channels = even_ref.shape[0] // 2, summed.shape[-1]
    for first, table, record in ((0, even_ref, summed), (near, odd_ref, differed)):
        result = jnp.dot(table[...], record[...], preferred_element_type=F32).astype(BF16)
        real, imag = result[:near], result[near:]
        spectra[0, s, first : first + near, :channels] = real
        spectra[0, s, first : first + near, channels:] = imag
        spectra[1, s, first : first + near, :channels] = imag
        spectra[1, s, first : first + near, channels:] = -real


def exchange_lanes(blocks):
    blocks = list(blocks)
    index = lax.broadcasted_iota(jnp.int32, blocks[0].shape, 1) // BLOCK
    for bit in (1, 2, 4):
        upper = (index & bit) != 0
        for i in range(8):
            if i & bit:
                continue
            first, second = blocks[i], blocks[i + bit]
            shift = BLOCK * bit
            blocks[i] = jnp.where(upper, pltpu.roll(second, shift, axis=1), first)
            blocks[i + bit] = jnp.where(upper, second, pltpu.roll(first, LANES - shift, axis=1))
    return blocks


def detect_kernel(
    record_hbm, tmpl_hbm, even_hbm, odd_hbm, high_hbm, low_hbm, cos_ref, sin_ref, weight_ref, out_ref,
    record, tmpl, even, odd, high, low, summed, differed, spectra, diagonal, cross, sems,
):
    pieces, late, piece, channels = record_hbm.shape
    templates, segments, length = weight_ref.shape
    bins = length // 2
    lanes = templates * BLOCK
    group = summed.shape[0]

    def load(s):
        return pltpu.make_async_copy(record_hbm.at[:, s], record.at[s], sems.at[s])

    tables_in = [
        pltpu.make_async_copy(even_hbm, even, sems.at[late]),
        pltpu.make_async_copy(odd_hbm, odd, sems.at[late + 1]),
    ]
    later_in = [
        pltpu.make_async_copy(tmpl_hbm, tmpl, sems.at[late + 2]),
        pltpu.make_async_copy(high_hbm, high, sems.at[late + 3]),
        pltpu.make_async_copy(low_hbm, low, sems.at[late + 4]),
    ]
    load(0).start()
    for copy in tables_in:
        copy.start()
    for s in range(1, late):
        load(s).start()
    for copy in later_in:
        copy.start()
    for copy in tables_in:
        copy.wait()

    @pl.loop(0, late // group)
    def _(i):
        for u in range(group):
            s = i * group + u
            load(s).wait()
            first = record[s, : pieces // 2].reshape(bins, channels)
            second = record[s, pieces // 2 :].reshape(bins, channels)
            summed[u] = first + second
            differed[u] = first - second
            store_spectra(spectra, s, even, odd, summed.at[u], differed.at[u])

    later_in[0].wait()
    rows = 2 * segments * BLOCK
    keep = (
        lax.broadcasted_iota(jnp.int32, (rows, lanes), 0) % BLOCK
        == lax.broadcasted_iota(jnp.int32, (rows, lanes), 1) % BLOCK
    )

    @pl.loop(0, bins // BLOCK // 4)
    def _(i):
        for u in range(4):
            b = i * 4 + u
            start = pl.multiple_of(b * BLOCK, BLOCK)
            left = spectra[:, :, pl.ds(start, BLOCK), :].reshape(rows, 2 * channels)
            right = tmpl[b].reshape(lanes, 2 * channels)
            product = lax.dot_general(
                left, right, (((1,), (1,)), ((), ())), preferred_element_type=F32
            )
            product = jnp.where(keep, product, 0.0).reshape(2 * segments, BLOCK, lanes)
            diagonal[b] = jnp.sum(product, axis=1)

    for g in range(bins // LANES):
        for j in range(lanes // LANES):
            blocks = [diagonal[g * 8 + i, :, j * LANES : (j + 1) * LANES] for i in range(8)]
            for i, block in enumerate(exchange_lanes(blocks)):
                cross[j * 8 + i, :, g * LANES : (g + 1) * LANES] = block

    real, imag = cross[:, :segments, :], cross[:, segments:, :]
    cosine, sine = cos_ref[...][None], sin_ref[...][None]
    total = templates * segments
    delayed = jnp.concatenate(
        [
            (real * cosine + imag * sine).reshape(total, bins),
            (imag * cosine - real * sine).reshape(total, bins),
        ],
        axis=1,
    )
    delayed_high = delayed.astype(BF16)
    delayed_low = (delayed - delayed_high.astype(F32)).astype(BF16)
    later_in[1].wait()
    later_in[2].wait()
    both = jnp.dot(
        jnp.concatenate([delayed_high, delayed_low], axis=0), high[...], preferred_element_type=F32
    )
    result = both[:total] + both[total:]
    result = result + jnp.dot(delayed_high, low[...], preferred_element_type=F32)
    scores = result.reshape(templates, segments, length) * weight_ref[...]
    stack = jnp.sum(scores, axis=1)
    for j in range(length // LANES):
        out_ref[j] = stack[:, j * LANES : (j + 1) * LANES]


def detect(record, tmpl, even, odd, high, low, cosine, sine, weights):
    pieces, late, piece, channels = record.shape
    templates, segments, length = weights.shape
    bins = length // 2
    vmem = pl.BlockSpec(memory_space=pltpu.VMEM)
    anywhere = pl.BlockSpec(memory_space=pl.ANY)
    group = 4
    return pl.pallas_call(
        detect_kernel,
        in_specs=[anywhere] * 6 + [vmem] * 3,
        out_specs=vmem,
        out_shape=jax.ShapeDtypeStruct((length // LANES, templates, LANES), F32),
        scratch_shapes=[
            pltpu.VMEM((late, pieces, piece, channels), BF16),
            pltpu.VMEM(tmpl.shape, BF16),
            pltpu.VMEM(even.shape, BF16),
            pltpu.VMEM(odd.shape, BF16),
            pltpu.VMEM(high.shape, BF16),
            pltpu.VMEM(low.shape, BF16),
            pltpu.VMEM((group, bins, channels), BF16),
            pltpu.VMEM((group, bins, channels), BF16),
            pltpu.VMEM((2, late, bins, 2 * channels), BF16),
            pltpu.VMEM((bins // BLOCK, 2 * segments, templates * BLOCK), F32),
            pltpu.VMEM((templates, 2 * segments, bins), F32),
            pltpu.SemaphoreType.DMA((late + 5,)),
        ],
        compiler_params=pltpu.CompilerParams(vmem_limit_bytes=54 << 20),
        cost_estimate=pl.CostEstimate(flops=12_000_000_000, bytes_accessed=24 << 20, transcendentals=0),
        name="detect",
    )(record, tmpl, even, odd, high, low, cosine, sine, weights)


def send(value, axis, move):
    return lax.ppermute(value, axis, [(i, move(i)) for i in range(lax.axis_size(axis))])


def body(samples, template_spectra, lag_lengths, offsets):
    segments, channels, piece = samples.shape
    chan_groups = lax.axis_size("chan")
    tmpl_groups = lax.axis_size("tmpl")
    channel_total = channels * chan_groups
    length = piece * tmpl_groups
    bins = length // 2
    templates = template_spectra.shape[1]
    me = lax.axis_index("tmpl")

    record = lax.all_gather(jnp.transpose(samples, (0, 2, 1)), "tmpl", axis=0, tiled=False)

    wide = samples.astype(F32)
    energy = jnp.sum(wide * wide, axis=1)
    tmpl, level = prepare_templates(template_spectra)
    level = jnp.sum(level, axis=1, keepdims=True) * (2.0 / length)
    sums = jnp.concatenate([energy, level], axis=1)
    for bit in (1, 2, 4):
        sums = sums + send(sums, "chan", lambda i: i ^ bit)
    energy = sums[:, :piece]
    level = sums[:, piece]
    for bit in (1, 2, 4, 8):
        other = send(energy, "tmpl", lambda i: i ^ bit)
        upper = (me & bit) != 0
        energy = jnp.concatenate(
            [jnp.where(upper, other, energy), jnp.where(upper, energy, other)], axis=1
        )
    weights = score_weights(lag_lengths, offsets, level, energy, channel_total)

    order = bin_order(bins).astype(np.int32)
    phase = offsets[:, None] * order[None, :] % length
    angle = phase.astype(F32) * (2.0 * math.pi / length)
    cosine, sine = jnp.cos(angle), jnp.sin(angle)
    even, odd, high, low = tables(length)
    partial = detect(record, tmpl, even, odd, high, low, cosine, sine, weights)
    return jnp.sum(lax.all_to_all(partial, "chan", 0, 0, tiled=False), axis=0)


def solution(mesh):
    return jax.shard_map(
        body,
        mesh=mesh,
        in_specs=(P(None, "chan", "tmpl"), P(None, "tmpl", "chan", None), P("tmpl"), P()),
        out_specs=P("tmpl", "chan"),
        check_vma=False,
    )
```

```python
import math

import jax
import jax.numpy as jnp
import numpy as np
from jax import lax
from jax.experimental import pallas as pl
from jax.experimental.pallas import tpu as pltpu
from jax.sharding import PartitionSpec as P

epsilon = 1e-06
LANES = 128
BLOCK = 16
F32 = jnp.float32
BF16 = jnp.bfloat16


def bin_order(bins):
    return np.concatenate([np.arange(0, bins, 2), np.arange(1, bins, 2)])


def tables(length):
    bins = length // 2
    angle = 2.0 * np.pi * (np.outer(bin_order(bins), np.arange(length)) % length) / length
    cosine, sine = np.cos(angle), -np.sin(angle)
    near = bins // 2
    even = np.concatenate([cosine[:near, :bins], sine[:near, :bins]], axis=0)
    odd = np.concatenate([cosine[near:, :bins], sine[near:, :bins]], axis=0)
    backward = np.concatenate([cosine, sine], axis=0) * (2.0 / length)
    high = backward.astype(BF16)
    low = (backward - high.astype(np.float64)).astype(BF16)
    return even.astype(BF16), odd.astype(BF16), high, low


def turn(bins):
    return (np.arange(bins)[None, :] == bin_order(bins)[:, None]).astype(BF16)


def template_kernel(turn_ref, g_ref, out_ref, energy_ref):
    step, channels, bins = g_ref.shape[1:]
    block = turn_ref.shape[0]
    for t in range(step):
        total = jnp.zeros((8, bins), F32)
        for part in range(2):
            wide = g_ref[part, t].astype(F32)
            total = total + jnp.sum((wide * wide).reshape(channels // 8, 8, bins), axis=0)
            for j in range(bins // block):
                rows = lax.dot_general(
                    turn_ref[...], g_ref[part, t, :, j * block : (j + 1) * block],
                    (((1,), (1,)), ((), ())), preferred_element_type=F32,
                ).astype(BF16)
                half = block // 2 // BLOCK
                for parity in range(2):
                    first = parity * (bins // 2 // BLOCK) + j * half
                    out_ref[first : first + half, t, :, part * channels : (part + 1) * channels] = (
                        rows[parity * block // 2 : (parity + 1) * block // 2].reshape(half, BLOCK, channels)
                    )
        total = jnp.sum(total, axis=0, keepdims=True)
        folded = total[:, :LANES]
        for j in range(1, bins // LANES):
            folded = folded + total[:, j * LANES : (j + 1) * LANES]
        energy_ref[pl.ds(pl.program_id(0) * step + t, 1), :] = folded


def prepare_templates(template_spectra):
    _, templates, channels, bins = template_spectra.shape
    step = 4
    matrix = turn(256)
    return pl.pallas_call(
        template_kernel,
        grid=(templates // step,),
        in_specs=[
            pl.BlockSpec(matrix.shape, lambda t: (0, 0)),
            pl.BlockSpec((2, step, channels, bins), lambda t: (0, t, 0, 0)),
        ],
        out_specs=[
            pl.BlockSpec((bins // BLOCK, step, BLOCK, 2 * channels), lambda t: (0, t, 0, 0)),
            pl.BlockSpec((templates, LANES), lambda t: (0, 0)),
        ],
        out_shape=[
            jax.ShapeDtypeStruct((bins // BLOCK, templates, BLOCK, 2 * channels), BF16),
            jax.ShapeDtypeStruct((templates, LANES), F32),
        ],
        compiler_params=pltpu.CompilerParams(vmem_limit_bytes=56 << 20),
        cost_estimate=pl.CostEstimate(flops=2_200_000_000, bytes_accessed=16 << 20, transcendentals=0),
        name="template_flip",
    )(matrix, template_spectra)


def weight_kernel(channel_total, scale, lag_ref, offset_ref, level_ref, energy_ref, out_ref, prefix):
    segments, length = energy_ref.shape
    templates = out_ref.shape[0]
    row = lax.broadcasted_iota(jnp.int32, (segments, length), 0)
    energy = energy_ref[...]
    delayed = jnp.zeros((segments, length), F32)
    for s in range(segments):
        delayed = jnp.where(row == s, pltpu.roll(energy, offset_ref[s], axis=1), delayed)
    before = lax.broadcasted_iota(jnp.int32, (LANES, LANES), 0) < lax.broadcasted_iota(
        jnp.int32, (LANES, LANES), 1
    )
    before = before.astype(F32)
    carry = jnp.zeros((segments, 1), F32)
    blocks = length // LANES
    for j in range(blocks):
        piece = delayed[:, j * LANES : (j + 1) * LANES]
        prefix[:, j * LANES : (j + 1) * LANES] = carry + jnp.dot(
            piece, before, precision=lax.Precision.HIGHEST, preferred_element_type=F32
        )
        carry = carry + jnp.sum(piece, axis=1, keepdims=True)
    first = prefix[:, :length]
    prefix[:, length : 2 * length] = first + carry
    prefix[:, 2 * length :] = first[:, :LANES] + 2.0 * carry
    span = length + LANES
    for t in range(templates):
        lag = lag_ref[t]
        start = pl.multiple_of((lag // LANES) * LANES, LANES)
        ahead = pltpu.roll(prefix[:, pl.ds(start, span)], span - lag % LANES, axis=1)[:, :length]
        power = (ahead - first) / (channel_total * lag.astype(F32))
        out_ref[t] = scale * lax.rsqrt(level_ref[t] * power + epsilon)


def score_weights(lag_lengths, offsets, level, energy, channel_total):
    segments, length = energy.shape
    templates = lag_lengths.shape[0]
    smem = pl.BlockSpec(memory_space=pltpu.SMEM)
    vmem = pl.BlockSpec(memory_space=pltpu.VMEM)

    def kernel(*refs):
        weight_kernel(channel_total, 1.0 / math.sqrt(segments), *refs)

    return pl.pallas_call(
        kernel,
        in_specs=[smem, smem, smem, vmem],
        out_specs=vmem,
        out_shape=jax.ShapeDtypeStruct((templates, segments, length), F32),
        scratch_shapes=[pltpu.VMEM((segments, 2 * length + LANES), F32)],
        compiler_params=pltpu.CompilerParams(vmem_limit_bytes=16 << 20),
        cost_estimate=pl.CostEstimate(flops=20_000_000, bytes_accessed=2 << 20, transcendentals=262144),
        name="score_weights",
    )(lag_lengths, offsets, level, energy)


def store_spectra(spectra, s, even_ref, odd_ref, summed, differed):
    near, channels = even_ref.shape[0] // 2, summed.shape[-1]
    for first, table, record in ((0, even_ref, summed), (near, odd_ref, differed)):
        result = jnp.dot(table[...], record[...], preferred_element_type=F32).astype(BF16)
        real, imag = result[:near], result[near:]
        spectra[0, s, first : first + near, :channels] = real
        spectra[0, s, first : first + near, channels:] = imag
        spectra[1, s, first : first + near, :channels] = imag
        spectra[1, s, first : first + near, channels:] = -real


def exchange_lanes(blocks):
    blocks = list(blocks)
    index = lax.broadcasted_iota(jnp.int32, blocks[0].shape, 1) // BLOCK
    for bit in (1, 2, 4):
        upper = (index & bit) != 0
        for i in range(8):
            if i & bit:
                continue
            first, second = blocks[i], blocks[i + bit]
            shift = BLOCK * bit
            blocks[i] = jnp.where(upper, pltpu.roll(second, shift, axis=1), first)
            blocks[i + bit] = jnp.where(upper, second, pltpu.roll(first, LANES - shift, axis=1))
    return blocks


def detect_kernel(
    own, own_c, own_x, own_xc, far, far_c, far_x, far_xc, beside, beside_c, beside_x, beside_xc,
    place_ref, tmpl_hbm, even_hbm, odd_hbm, out_ref,
    held, tmpl, even_ref, odd_ref, summed, differed, spectra, diagonal, sems, piece_sems,
):
    segments, piece, channels = own.shape
    templates, _, bins = out_ref.shape
    lanes = templates * BLOCK
    group = summed.shape[0]
    group = held.shape[1]
    sources = [
        (own, 0), (own_c, 0), (own_x, 0), (own_xc, 0),
        (beside, 0), (beside, 1), (beside_x, 0), (beside_x, 1),
        (far, 0), (far_c, 0), (far_x, 0), (far_xc, 0),
        (beside_c, 1), (beside_c, 0), (beside_xc, 1), (beside_xc, 0),
    ]

    def fetch(i):
        return [
            pltpu.make_async_copy(
                ref.at[pl.ds(k * segments + i * group, group)], held.at[j, i], piece_sems.at[i, j]
            )
            for j, (ref, k) in enumerate(sources)
        ]

    tables_in = [
        pltpu.make_async_copy(even_hbm, even_ref, sems.at[0]),
        pltpu.make_async_copy(odd_hbm, odd_ref, sems.at[1]),
    ]
    copy = pltpu.make_async_copy(tmpl_hbm, tmpl, sems.at[2])
    rounds = segments // group
    for started in fetch(0) + tables_in:
        started.start()
    for i in range(1, rounds):
        for started in fetch(i):
            started.start()
    copy.start()

    pairs = len(sources) // 2
    starts = [pl.multiple_of(place_ref[k], piece) for k in range(pairs)]
    signs = [place_ref[pairs + k].astype(F32).astype(BF16) for k in range(pairs)]
    for started in tables_in:
        started.wait()

    @pl.loop(0, rounds)
    def _(i):
        for started in fetch(i):
            started.wait()
        for u in range(group):
            for k in range(pairs):
                first, second = held[k, i, u], held[pairs + k, i, u]
                summed[u, pl.ds(starts[k], piece), :] = first + second
                differed[u, pl.ds(starts[k], piece), :] = (first - second) * signs[k]
            store_spectra(spectra, i * group + u, even_ref, odd_ref, summed.at[u], differed.at[u])

    copy.wait()
    rows = 2 * segments * BLOCK
    keep = (
        lax.broadcasted_iota(jnp.int32, (rows, lanes), 0) % BLOCK
        == lax.broadcasted_iota(jnp.int32, (rows, lanes), 1) % BLOCK
    )

    @pl.loop(0, bins // BLOCK // 4)
    def _(i):
        for u in range(4):
            b = i * 4 + u
            start = pl.multiple_of(b * BLOCK, BLOCK)
            left = spectra[:, :, pl.ds(start, BLOCK), :].reshape(rows, 2 * channels)
            right = tmpl[b].reshape(lanes, 2 * channels)
            product = lax.dot_general(
                left, right, (((1,), (1,)), ((), ())), preferred_element_type=F32
            )
            product = jnp.where(keep, product, 0.0).reshape(2 * segments, BLOCK, lanes)
            diagonal[b] = jnp.sum(product, axis=1)

    for g in range(bins // LANES):
        for j in range(lanes // LANES):
            blocks = [diagonal[g * 8 + i, :, j * LANES : (j + 1) * LANES] for i in range(8)]
            for i, block in enumerate(exchange_lanes(blocks)):
                out_ref[j * 8 + i, :, g * LANES : (g + 1) * LANES] = block


def score_kernel(cross, high, low, cos_ref, sin_ref, weight_ref, out_ref):
    templates, segments, length = weight_ref.shape
    bins = length // 2
    real, imag = cross[:, :segments, :], cross[:, segments:, :]
    cosine, sine = cos_ref[...][None], sin_ref[...][None]
    total = templates * segments
    delayed = jnp.concatenate(
        [
            (real * cosine + imag * sine).reshape(total, bins),
            (imag * cosine - real * sine).reshape(total, bins),
        ],
        axis=1,
    )
    delayed_high = delayed.astype(BF16)
    delayed_low = (delayed - delayed_high.astype(F32)).astype(BF16)
    both = jnp.dot(
        jnp.concatenate([delayed_high, delayed_low], axis=0), high[...], preferred_element_type=F32
    )
    result = both[:total] + both[total:]
    result = result + jnp.dot(delayed_high, low[...], preferred_element_type=F32)
    scores = result.reshape(templates, segments, length) * weight_ref[...]
    stack = jnp.sum(scores, axis=1)
    for j in range(length // LANES):
        out_ref[j] = stack[:, j * LANES : (j + 1) * LANES]


def cross_spectra(pieces, place, tmpl, even, odd):
    segments, piece, channels = pieces[0].shape
    templates = tmpl.shape[1]
    bins = even.shape[0]
    vmem = pl.BlockSpec(memory_space=pltpu.VMEM)
    anywhere = pl.BlockSpec(memory_space=pl.ANY)
    group = 4
    return pl.pallas_call(
        detect_kernel,
        in_specs=[anywhere] * len(pieces) + [pl.BlockSpec(memory_space=pltpu.SMEM)] + [anywhere] * 3,
        out_specs=vmem,
        out_shape=jax.ShapeDtypeStruct((templates, 2 * segments, bins), F32),
        scratch_shapes=[
            pltpu.VMEM((16, segments // group, group, piece, channels), BF16),
            pltpu.VMEM(tmpl.shape, BF16),
            pltpu.VMEM(even.shape, BF16),
            pltpu.VMEM(odd.shape, BF16),
            pltpu.VMEM((group, bins, channels), BF16),
            pltpu.VMEM((group, bins, channels), BF16),
            pltpu.VMEM((2, segments, bins, 2 * channels), BF16),
            pltpu.VMEM((bins // BLOCK, 2 * segments, templates * BLOCK), F32),
            pltpu.SemaphoreType.DMA((3,)),
            pltpu.SemaphoreType.DMA((segments // group, 16)),
        ],
        compiler_params=pltpu.CompilerParams(vmem_limit_bytes=58 << 20),
        cost_estimate=pl.CostEstimate(flops=12_000_000_000, bytes_accessed=24 << 20, transcendentals=0),
        name="cross_spectra",
    )(*pieces, place, tmpl, even, odd)


def score(cross, high, low, cosine, sine, weights):
    templates, _, length = weights.shape
    vmem = pl.BlockSpec(memory_space=pltpu.VMEM)
    return pl.pallas_call(
        score_kernel,
        in_specs=[vmem] * 6,
        out_specs=vmem,
        out_shape=jax.ShapeDtypeStruct((length // LANES, templates, LANES), F32),
        compiler_params=pltpu.CompilerParams(vmem_limit_bytes=24 << 20),
        cost_estimate=pl.CostEstimate(flops=2_000_000_000, bytes_accessed=6 << 20, transcendentals=0),
        name="score",
    )(cross, high, low, cosine, sine, weights)


def send(value, axis, move):
    return lax.ppermute(value, axis, [(i, move(i)) for i in range(lax.axis_size(axis))])


def apart(i):
    return (i + (-4 if i % 2 else 4)) % 16


def across(i):
    return i ^ 2


def sibling(i):
    return i ^ 1


def after(value, *earlier):
    return lax.optimization_barrier((value, *earlier))[0]


def body(samples, template_spectra, lag_lengths, offsets):
    segments, channels, piece = samples.shape
    chan_groups = lax.axis_size("chan")
    tmpl_groups = lax.axis_size("tmpl")
    channel_total = channels * chan_groups
    length = piece * tmpl_groups
    bins = length // 2
    templates = template_spectra.shape[1]
    me = lax.axis_index("tmpl")

    wide = samples.astype(F32)
    energy = jnp.sum(wide * wide, axis=1)

    def double(energy, bit):
        other = send(energy, "tmpl", lambda i: i ^ bit)
        upper = (me & bit) != 0
        return jnp.concatenate(
            [jnp.where(upper, other, energy), jnp.where(upper, energy, other)], axis=1
        )

    fence = lax.optimization_barrier
    own = jnp.transpose(samples, (0, 2, 1))
    own_c = send(own, "tmpl", sibling)
    beside = send(jnp.concatenate([own, own_c], axis=0), "tmpl", apart)
    energy = double(double(energy, 1), 2)
    own_x = send(after(own, energy), "tmpl", across)
    tmpl, level = prepare_templates(after(template_spectra, energy))
    level = jnp.sum(level, axis=1, keepdims=True) * (2.0 / length)
    energy = double(energy, 4)
    beside, tmpl, level, energy = fence((beside, tmpl, level, energy))

    far = send(beside[:segments], "tmpl", apart)
    beside_c = send(beside, "tmpl", sibling)
    energy = double(energy, 8)
    sums = jnp.concatenate([energy, jnp.broadcast_to(level, (templates, LANES))], axis=1)
    sums = sums + send(sums, "chan", lambda i: i ^ 4)
    own_xc = send(after(own_x, beside), "tmpl", sibling)
    beside_x = send(after(jnp.concatenate([own_x, own_xc], axis=0), energy), "tmpl", apart)
    far, sums = fence((far, sums))
    far_x = send(far, "tmpl", across)
    far_c = send(far, "tmpl", sibling)
    sums = sums + send(sums, "chan", lambda i: i ^ 1)
    sums = sums + send(sums, "chan", lambda i: i ^ 2)
    energy, level = sums[:, :length], sums[:, length]
    weights = score_weights(lag_lengths, offsets, level, energy, channel_total)
    beside_x, far_x, far_c, weights = fence((beside_x, far_x, far_c, weights))
    beside_xc = send(beside_x, "tmpl", sibling)
    far_xc = send(far_x, "tmpl", sibling)

    order = bin_order(bins).astype(np.int32)
    phase = offsets[:, None] * order[None, :] % length
    angle = phase.astype(F32) * (2.0 * math.pi / length)
    cosine, sine = jnp.cos(angle), jnp.sin(angle)
    even, odd, high, low = tables(length)

    k = lax.iota(jnp.int32, 8)
    z = (me // 4 + jnp.where(k < 4, 0, 2 * (me % 2) - 1)) % 4
    start = (z % 2 * 4 + ((me ^ k) & 3)) * piece
    place = jnp.concatenate([start, jnp.where(z < 2, 1, -1)]).astype(jnp.int32)
    pieces = (
        own, own_c, own_x, own_xc, far, far_c, far_x, far_xc, beside, beside_c, beside_x, beside_xc,
    )
    cross = cross_spectra(pieces, place, tmpl, even, odd)
    partial = score(cross, high, low, cosine, sine, weights)
    return jnp.sum(lax.all_to_all(partial, "chan", 0, 0, tiled=False), axis=0)


def solution(mesh):
    return jax.shard_map(
        body,
        mesh=mesh,
        in_specs=(P(None, "chan", "tmpl"), P(None, "tmpl", "chan", None), P("tmpl"), P()),
        out_specs=P("tmpl", "chan"),
        check_vma=False,
    )
```

```python
import math

import jax
import jax.numpy as jnp
import numpy as np
from jax import lax
from jax.experimental import pallas as pl
from jax.experimental.pallas import tpu as pltpu
from jax.sharding import PartitionSpec as P

epsilon = 1e-06
LANES = 128
BLOCK = 16
F32 = jnp.float32
BF16 = jnp.bfloat16


def bin_order(bins):
    return np.concatenate([np.arange(0, bins, 2), np.arange(1, bins, 2)])


def tables(length):
    bins = length // 2
    angle = 2.0 * np.pi * (np.outer(bin_order(bins), np.arange(length)) % length) / length
    cosine, sine = np.cos(angle), -np.sin(angle)
    near = bins // 2
    even = np.concatenate([cosine[:near, :bins], sine[:near, :bins]], axis=0)
    odd = np.concatenate([cosine[near:, :bins], sine[near:, :bins]], axis=0)
    backward = np.concatenate([cosine, sine], axis=0) * (2.0 / length)
    return np.stack([even, odd]).astype(BF16), backward.astype(BF16)


def turn(bins):
    return (np.arange(bins)[None, :] == bin_order(bins)[:, None]).astype(BF16)


def template_kernel(turn_ref, g_ref, out_ref, energy_ref):
    step, channels, bins = g_ref.shape[1:]
    block = turn_ref.shape[0]
    for t in range(step):
        total = jnp.zeros((8, bins), F32)
        for part in range(2):
            wide = g_ref[part, t].astype(F32)
            total = total + jnp.sum((wide * wide).reshape(channels // 8, 8, bins), axis=0)
            for j in range(bins // block):
                rows = lax.dot_general(
                    turn_ref[...], g_ref[part, t, :, j * block : (j + 1) * block],
                    (((1,), (1,)), ((), ())), preferred_element_type=F32,
                ).astype(BF16)
                half = block // 2 // BLOCK
                for parity in range(2):
                    first = parity * (bins // 2 // BLOCK) + j * half
                    out_ref[first : first + half, t, :, part * channels : (part + 1) * channels] = (
                        rows[parity * block // 2 : (parity + 1) * block // 2].reshape(half, BLOCK, channels)
                    )
        level = jnp.sum(jnp.sum(total, axis=0, keepdims=True), axis=1, keepdims=True) * (1.0 / bins)
        energy_ref[pl.ds(pl.program_id(0) * step + t, 1), :] = jnp.broadcast_to(level, (1, LANES))


def prepare_templates(template_spectra):
    _, templates, channels, bins = template_spectra.shape
    step = 4
    matrix = turn(256)
    return pl.pallas_call(
        template_kernel,
        grid=(templates // step,),
        in_specs=[
            pl.BlockSpec(matrix.shape, lambda t: (0, 0)),
            pl.BlockSpec((2, step, channels, bins), lambda t: (0, t, 0, 0)),
        ],
        out_specs=[
            pl.BlockSpec((bins // BLOCK, step, BLOCK, 2 * channels), lambda t: (0, t, 0, 0)),
            pl.BlockSpec((templates, LANES), lambda t: (0, 0)),
        ],
        out_shape=[
            jax.ShapeDtypeStruct((bins // BLOCK, templates, BLOCK, 2 * channels), BF16),
            jax.ShapeDtypeStruct((templates, LANES), F32),
        ],
        compiler_params=pltpu.CompilerParams(vmem_limit_bytes=56 << 20),
        cost_estimate=pl.CostEstimate(flops=2_200_000_000, bytes_accessed=16 << 20, transcendentals=0),
        name="template_flip",
    )(matrix, template_spectra)


def weight_kernel(channel_total, scale, lag_ref, offset_ref, level_ref, energy_ref, out_ref, prefix):
    segments, length = energy_ref.shape
    templates = out_ref.shape[0]
    row = lax.broadcasted_iota(jnp.int32, (segments, length), 0)
    energy = energy_ref[...]
    delayed = jnp.zeros((segments, length), F32)
    for s in range(segments):
        delayed = jnp.where(row == s, pltpu.roll(energy, offset_ref[s], axis=1), delayed)
    before = lax.broadcasted_iota(jnp.int32, (LANES, LANES), 0) < lax.broadcasted_iota(
        jnp.int32, (LANES, LANES), 1
    )
    before = before.astype(F32)
    carry = jnp.zeros((segments, 1), F32)
    blocks = length // LANES
    for j in range(blocks):
        piece = delayed[:, j * LANES : (j + 1) * LANES]
        prefix[:, j * LANES : (j + 1) * LANES] = carry + jnp.dot(
            piece, before, precision=lax.Precision.HIGHEST, preferred_element_type=F32
        )
        carry = carry + jnp.sum(piece, axis=1, keepdims=True)
    first = prefix[:, :length]
    prefix[:, length : 2 * length] = first + carry
    prefix[:, 2 * length :] = first[:, :LANES] + 2.0 * carry
    span = length + LANES
    for t in range(templates):
        lag = lag_ref[t]
        start = pl.multiple_of((lag // LANES) * LANES, LANES)
        ahead = pltpu.roll(prefix[:, pl.ds(start, span)], span - lag % LANES, axis=1)[:, :length]
        power = (ahead - first) / (channel_total * lag.astype(F32))
        out_ref[t] = scale * lax.rsqrt(level_ref[t] * power + epsilon)


def store_spectra(spectra, s, forward, summed, differed):
    near, channels = forward.shape[1] // 2, summed.shape[-1]
    for parity, record in enumerate((summed, differed)):
        first = parity * near
        result = jnp.dot(forward[parity], record[...], preferred_element_type=F32).astype(BF16)
        real, imag = result[:near], result[near:]
        spectra[0, s, first : first + near, :channels] = real
        spectra[0, s, first : first + near, channels:] = imag
        spectra[1, s, first : first + near, :channels] = imag
        spectra[1, s, first : first + near, channels:] = -real


def exchange_lanes(blocks):
    blocks = list(blocks)
    index = lax.broadcasted_iota(jnp.int32, blocks[0].shape, 1) // BLOCK
    for bit in (1, 2, 4):
        upper = (index & bit) != 0
        for i in range(8):
            if i & bit:
                continue
            first, second = blocks[i], blocks[i + bit]
            shift = BLOCK * bit
            blocks[i] = jnp.where(upper, pltpu.roll(second, shift, axis=1), first)
            blocks[i + bit] = jnp.where(upper, second, pltpu.roll(first, LANES - shift, axis=1))
    return blocks


def detect_kernel(channel_total, *refs):
    sources, refs = refs[:16], refs[16:]
    lag_ref, offset_ref, level_ref, place_ref, energy_ref = refs[:5]
    forward_hbm, tmpl_hbm, back_hbm, cos_ref, sin_ref, out_ref = refs[5:11]
    forward, tmpl, back, weights, prefix, summed, differed, spectra, diagonal, cross, sems = refs[11:]
    segments, piece, channels = sources[0].shape
    templates, _, length = weights.shape
    bins = length // 2
    lanes = templates * BLOCK
    group = summed.shape[0]
    tables_in = [
        pltpu.make_async_copy(source, target, sems.at[j])
        for j, (source, target) in enumerate(
            ((forward_hbm, forward), (back_hbm, back))
        )
    ]
    copy_tmpl = pltpu.make_async_copy(tmpl_hbm, tmpl, sems.at[2])
    for copy in (tables_in[0], copy_tmpl, tables_in[1]):
        copy.start()
    weight_kernel(channel_total, 1.0 / math.sqrt(segments), lag_ref, offset_ref, level_ref, energy_ref, weights, prefix)

    pairs = len(sources) // 2
    starts = [pl.multiple_of(place_ref[k], piece) for k in range(pairs)]
    signs = [place_ref[pairs + k].astype(F32).astype(BF16) for k in range(pairs)]
    tables_in[0].wait()

    @pl.loop(0, segments // group)
    def _(i):
        for u in range(group):
            s = i * group + u
            for k in range(pairs):
                first, second = sources[k][s], sources[pairs + k][s]
                summed[u, pl.ds(starts[k], piece), :] = first + second
                differed[u, pl.ds(starts[k], piece), :] = (first - second) * signs[k]
            store_spectra(spectra, s, forward, summed.at[u], differed.at[u])

    copy_tmpl.wait()
    rows = 2 * segments * BLOCK
    keep = (
        lax.broadcasted_iota(jnp.int32, (rows, lanes), 0) % BLOCK
        == lax.broadcasted_iota(jnp.int32, (rows, lanes), 1) % BLOCK
    )

    @pl.loop(0, bins // BLOCK // 4)
    def _(i):
        for u in range(4):
            b = i * 4 + u
            start = pl.multiple_of(b * BLOCK, BLOCK)
            left = spectra[:, :, pl.ds(start, BLOCK), :].reshape(rows, 2 * channels)
            right = tmpl[b].reshape(lanes, 2 * channels)
            product = lax.dot_general(
                left, right, (((1,), (1,)), ((), ())), preferred_element_type=F32
            )
            product = jnp.where(keep, product, 0.0).reshape(2 * segments, BLOCK, lanes)
            diagonal[b] = jnp.sum(product, axis=1)

    for g in range(bins // LANES):
        for j in range(lanes // LANES):
            blocks = [diagonal[g * 8 + i, :, j * LANES : (j + 1) * LANES] for i in range(8)]
            for i, block in enumerate(exchange_lanes(blocks)):
                cross[j * 8 + i, :, g * LANES : (g + 1) * LANES] = block

    real, imag = cross[:, :segments, :], cross[:, segments:, :]
    cosine, sine = cos_ref[...][None], sin_ref[...][None]
    total = templates * segments
    delayed = jnp.concatenate(
        [
            (real * cosine + imag * sine).reshape(total, bins),
            (imag * cosine - real * sine).reshape(total, bins),
        ],
        axis=1,
    )
    delayed_high = delayed.astype(BF16)
    delayed_low = (delayed - delayed_high.astype(F32)).astype(BF16)
    tables_in[1].wait()
    both = jnp.dot(
        jnp.concatenate([delayed_high, delayed_low], axis=0), back[...], preferred_element_type=F32
    )
    result = both[:total] + both[total:]
    scores = result.reshape(templates, segments, length) * weights[...]
    stack = jnp.sum(scores, axis=1)
    for j in range(length // LANES):
        out_ref[j] = stack[:, j * LANES : (j + 1) * LANES]


def detect(pieces, lag_lengths, offsets, level, place, energy, forward, tmpl, back, cosine, sine, channel_total):
    segments, piece, channels = pieces[0].shape
    templates, length = lag_lengths.shape[0], energy.shape[1]
    bins = length // 2
    vmem = pl.BlockSpec(memory_space=pltpu.VMEM)
    smem = pl.BlockSpec(memory_space=pltpu.SMEM)
    anywhere = pl.BlockSpec(memory_space=pl.ANY)
    group = 4

    def kernel(*refs):
        detect_kernel(channel_total, *refs)

    return pl.pallas_call(
        kernel,
        in_specs=[vmem] * len(pieces) + [smem] * 4 + [vmem] + [anywhere] * 3 + [vmem] * 2,
        out_specs=vmem,
        out_shape=jax.ShapeDtypeStruct((length // LANES, templates, LANES), F32),
        scratch_shapes=[
            pltpu.VMEM(forward.shape, BF16),
            pltpu.VMEM(tmpl.shape, BF16),
            pltpu.VMEM(back.shape, BF16),
            pltpu.VMEM((templates, segments, length), F32),
            pltpu.VMEM((segments, 2 * length + LANES), F32),
            pltpu.VMEM((group, bins, channels), BF16),
            pltpu.VMEM((group, bins, channels), BF16),
            pltpu.VMEM((2, segments, bins, 2 * channels), BF16),
            pltpu.VMEM((bins // BLOCK, 2 * segments, templates * BLOCK), F32),
            pltpu.VMEM((templates, 2 * segments, bins), F32),
            pltpu.SemaphoreType.DMA((3,)),
        ],
        compiler_params=pltpu.CompilerParams(vmem_limit_bytes=44 << 20),
        cost_estimate=pl.CostEstimate(flops=12_000_000_000, bytes_accessed=24 << 20, transcendentals=0),
        name="detect",
    )(*pieces, lag_lengths, offsets, level, place, energy, forward, tmpl, back, cosine, sine)


def send(value, axis, move):
    return lax.ppermute(value, axis, [(i, move(i)) for i in range(lax.axis_size(axis))])


def apart(i):
    return (i + (-4 if i % 2 else 4)) % 16


def across(i):
    return i ^ 2


def sibling(i):
    return i ^ 1


def after(value, *earlier):
    return lax.optimization_barrier((value, *earlier))[0]


def body(samples, template_spectra, lag_lengths, offsets):
    segments, channels, piece = samples.shape
    chan_groups = lax.axis_size("chan")
    tmpl_groups = lax.axis_size("tmpl")
    channel_total = channels * chan_groups
    length = piece * tmpl_groups
    bins = length // 2
    templates = template_spectra.shape[1]
    me = lax.axis_index("tmpl")

    wide = samples.astype(F32)
    energy = jnp.sum(wide * wide, axis=1)

    def double(energy, bit, flip=0):
        other = send(energy, "tmpl", lambda i: i ^ bit ^ flip)
        upper = (me & bit) != 0
        return jnp.concatenate(
            [jnp.where(upper, other, energy), jnp.where(upper, energy, other)], axis=1
        )

    fence = lax.optimization_barrier
    own = jnp.transpose(samples, (0, 2, 1))
    beside_0 = send(own, "tmpl", apart)
    own_c = send(own, "tmpl", sibling)
    beside_1 = send(own_c, "tmpl", apart)
    energy = double(after(double(energy, 1), own_c), 2)
    own_x = send(own, "tmpl", across)
    energy_early = energy
    energy = double(energy, 4)
    far = send(beside_0, "tmpl", apart)
    tmpl, level = prepare_templates(after(template_spectra, energy_early))
    far, own_x, beside_1, level, energy = fence((far, own_x, beside_1, level, energy))

    far_x = send(far, "tmpl", across)
    energy = double(energy, 8, 4)
    own_xc = send(own_x, "tmpl", sibling)
    beside_0c, beside_1c = send(beside_0, "tmpl", sibling), send(beside_1, "tmpl", sibling)
    far_c = send(far, "tmpl", sibling)
    own_x, own_xc, energy = fence((own_x, own_xc, energy))
    beside_x0, beside_x1 = send(own_x, "tmpl", apart), send(own_xc, "tmpl", apart)
    sums = jnp.concatenate([energy, level], axis=1)
    sums = sums + send(sums, "chan", lambda i: i ^ 1)
    sums = sums + send(sums, "chan", lambda i: i ^ 3)
    sums = sums + send(sums, "chan", lambda i: i ^ 4)
    energy, level = sums[:, :length], sums[:, length]
    beside_x0c, beside_x1c = send(beside_x0, "tmpl", sibling), send(beside_x1, "tmpl", sibling)
    far_xc = send(far_x, "tmpl", sibling)

    order = bin_order(bins).astype(np.int32)
    phase = offsets[:, None] * order[None, :] % length
    angle = phase.astype(F32) * (2.0 * math.pi / length)
    cosine, sine = jnp.cos(angle), jnp.sin(angle)
    forward, back = tables(length)

    k = lax.iota(jnp.int32, 8)
    z = (me // 4 + jnp.where(k < 4, 0, 2 * (me % 2) - 1)) % 4
    start = (z % 2 * 4 + ((me ^ k) & 3)) * piece
    place = jnp.concatenate([start, jnp.where(z < 2, 1, -1)]).astype(jnp.int32)
    pieces = (
        own, own_c, own_x, own_xc, beside_0, beside_1, beside_x0, beside_x1,
        far, far_c, far_x, far_xc, beside_1c, beside_0c, beside_x1c, beside_x0c,
    )
    partial = detect(
        pieces, lag_lengths, offsets, level, place, energy, forward, tmpl, back, cosine, sine, channel_total
    )
    return jnp.sum(lax.all_to_all(partial, "chan", 0, 0, tiled=False), axis=0)


def solution(mesh):
    return jax.shard_map(
        body,
        mesh=mesh,
        in_specs=(P(None, "chan", "tmpl"), P(None, "tmpl", "chan", None), P("tmpl"), P()),
        out_specs=P("tmpl", "chan"),
        check_vma=False,
    )
```

```python
import math

import jax
import jax.numpy as jnp
import numpy as np
from jax import lax
from jax.experimental import pallas as pl
from jax.experimental.pallas import tpu as pltpu
from jax.sharding import PartitionSpec as P

epsilon = 1e-06
LANES = 128
BLOCK = 16
F32 = jnp.float32
BF16 = jnp.bfloat16


def bin_order(bins):
    return np.concatenate([np.arange(0, bins, 2), np.arange(1, bins, 2)])


def tables(length):
    bins = length // 2
    angle = 2.0 * np.pi * (np.outer(bin_order(bins), np.arange(length)) % length) / length
    cosine, sine = np.cos(angle), -np.sin(angle)
    near = bins // 2
    even = np.concatenate([cosine[:near, :bins], sine[:near, :bins]], axis=0)
    odd = np.concatenate([cosine[near:, :bins], sine[near:, :bins]], axis=0)
    backward = np.concatenate([cosine, sine], axis=0) * (2.0 / length)
    return np.stack([even, odd]).astype(BF16), backward.astype(BF16)


def turn(bins):
    return (np.arange(bins)[None, :] == bin_order(bins)[:, None]).astype(BF16)


def template_kernel(turn_ref, g_ref, out_ref, energy_ref):
    step, channels, bins = g_ref.shape[1:]
    block = turn_ref.shape[0]
    for t in range(step):
        total = jnp.zeros((8, bins), F32)
        for part in range(2):
            wide = g_ref[part, t].astype(F32)
            total = total + jnp.sum((wide * wide).reshape(channels // 8, 8, bins), axis=0)
            for j in range(bins // block):
                rows = lax.dot_general(
                    turn_ref[...], g_ref[part, t, :, j * block : (j + 1) * block],
                    (((1,), (1,)), ((), ())), preferred_element_type=F32,
                ).astype(BF16)
                half = block // 2 // BLOCK
                for parity in range(2):
                    first = parity * (bins // 2 // BLOCK) + j * half
                    out_ref[first : first + half, t, :, part * channels : (part + 1) * channels] = (
                        rows[parity * block // 2 : (parity + 1) * block // 2].reshape(half, BLOCK, channels)
                    )
        level = jnp.sum(jnp.sum(total, axis=0, keepdims=True), axis=1, keepdims=True) * (1.0 / bins)
        energy_ref[pl.ds(pl.program_id(0) * step + t, 1), :] = jnp.broadcast_to(level, (1, LANES))


def prepare_templates(template_spectra):
    _, templates, channels, bins = template_spectra.shape
    step = 4
    matrix = turn(256)
    return pl.pallas_call(
        template_kernel,
        grid=(templates // step,),
        in_specs=[
            pl.BlockSpec(matrix.shape, lambda t: (0, 0)),
            pl.BlockSpec((2, step, channels, bins), lambda t: (0, t, 0, 0)),
        ],
        out_specs=[
            pl.BlockSpec((bins // BLOCK, step, BLOCK, 2 * channels), lambda t: (0, t, 0, 0)),
            pl.BlockSpec((templates, LANES), lambda t: (0, 0)),
        ],
        out_shape=[
            jax.ShapeDtypeStruct((bins // BLOCK, templates, BLOCK, 2 * channels), BF16),
            jax.ShapeDtypeStruct((templates, LANES), F32),
        ],
        compiler_params=pltpu.CompilerParams(vmem_limit_bytes=56 << 20),
        cost_estimate=pl.CostEstimate(flops=2_200_000_000, bytes_accessed=16 << 20, transcendentals=0),
        name="template_flip",
    )(matrix, template_spectra)


def weight_kernel(channel_total, scale, lag_ref, offset_ref, level_ref, energy_ref, out_ref, prefix):
    segments, length = energy_ref.shape
    templates = out_ref.shape[0]
    row = lax.broadcasted_iota(jnp.int32, (segments, length), 0)
    energy = energy_ref[...]
    delayed = jnp.zeros((segments, length), F32)
    for s in range(segments):
        delayed = jnp.where(row == s, pltpu.roll(energy, offset_ref[s], axis=1), delayed)
    before = lax.broadcasted_iota(jnp.int32, (LANES, LANES), 0) < lax.broadcasted_iota(
        jnp.int32, (LANES, LANES), 1
    )
    before = before.astype(F32)
    carry = jnp.zeros((segments, 1), F32)
    blocks = length // LANES
    for j in range(blocks):
        piece = delayed[:, j * LANES : (j + 1) * LANES]
        prefix[:, j * LANES : (j + 1) * LANES] = carry + jnp.dot(
            piece, before, precision=lax.Precision.HIGHEST, preferred_element_type=F32
        )
        carry = carry + jnp.sum(piece, axis=1, keepdims=True)
    first = prefix[:, :length]
    prefix[:, length : 2 * length] = first + carry
    prefix[:, 2 * length :] = first[:, :LANES] + 2.0 * carry
    span = length + LANES
    for t in range(templates):
        lag = lag_ref[t]
        start = pl.multiple_of((lag // LANES) * LANES, LANES)
        ahead = pltpu.roll(prefix[:, pl.ds(start, span)], span - lag % LANES, axis=1)[:, :length]
        power = (ahead - first) / (channel_total * lag.astype(F32))
        out_ref[t] = scale * lax.rsqrt(level_ref[t] * power + epsilon)


def store_spectra(spectra, s, forward, summed, differed):
    near, channels = forward.shape[1] // 2, summed.shape[-1]
    for parity, record in enumerate((summed, differed)):
        first = parity * near
        result = jnp.dot(forward[parity], record[...], preferred_element_type=F32).astype(BF16)
        real, imag = result[:near], result[near:]
        spectra[0, s, first : first + near, :channels] = real
        spectra[0, s, first : first + near, channels:] = imag
        spectra[1, s, first : first + near, :channels] = imag
        spectra[1, s, first : first + near, channels:] = -real


def exchange_lanes(blocks):
    blocks = list(blocks)
    index = lax.broadcasted_iota(jnp.int32, blocks[0].shape, 1) // BLOCK
    for bit in (1, 2, 4):
        upper = (index & bit) != 0
        for i in range(8):
            if i & bit:
                continue
            first, second = blocks[i], blocks[i + bit]
            shift = BLOCK * bit
            blocks[i] = jnp.where(upper, pltpu.roll(second, shift, axis=1), first)
            blocks[i + bit] = jnp.where(upper, second, pltpu.roll(first, LANES - shift, axis=1))
    return blocks


def detect_kernel(channel_total, *refs):
    sources, refs = refs[:16], refs[16:]
    lag_ref, offset_ref, level_ref, place_ref, energy_ref = refs[:5]
    forward_hbm, tmpl_hbm, back_hbm, cos_ref, sin_ref, out_ref = refs[5:11]
    forward, tmpl, back, weights, prefix, summed, differed, spectra, diagonal, cross, sems = refs[11:]
    segments, piece, channels = sources[0].shape
    templates, _, length = weights.shape
    bins = length // 2
    lanes = templates * BLOCK
    group = summed.shape[0]
    tables_in = [
        pltpu.make_async_copy(source, target, sems.at[j])
        for j, (source, target) in enumerate(
            ((forward_hbm, forward), (back_hbm, back))
        )
    ]
    copy_tmpl = pltpu.make_async_copy(tmpl_hbm, tmpl, sems.at[2])
    for copy in (tables_in[0], copy_tmpl, tables_in[1]):
        copy.start()
    weight_kernel(channel_total, 1.0 / math.sqrt(segments), lag_ref, offset_ref, level_ref, energy_ref, weights, prefix)

    pairs = len(sources) // 2
    starts = [pl.multiple_of(place_ref[k], piece) for k in range(pairs)]
    signs = [place_ref[pairs + k].astype(F32).astype(BF16) for k in range(pairs)]
    tables_in[0].wait()

    @pl.loop(0, segments // group)
    def _(i):
        for u in range(group):
            s = i * group + u
            for k in range(pairs):
                first, second = sources[k][s], sources[pairs + k][s]
                summed[u, pl.ds(starts[k], piece), :] = first + second
                differed[u, pl.ds(starts[k], piece), :] = (first - second) * signs[k]
            store_spectra(spectra, s, forward, summed.at[u], differed.at[u])

    copy_tmpl.wait()
    rows = 2 * segments * BLOCK
    keep = (
        lax.broadcasted_iota(jnp.int32, (rows, lanes), 0) % BLOCK
        == lax.broadcasted_iota(jnp.int32, (rows, lanes), 1) % BLOCK
    )

    @pl.loop(0, bins // BLOCK // 16)
    def _(i):
        for u in range(16):
            b = i * 16 + u
            start = pl.multiple_of(b * BLOCK, BLOCK)
            left = spectra[:, :, pl.ds(start, BLOCK), :].reshape(rows, 2 * channels)
            right = tmpl[b].reshape(lanes, 2 * channels)
            product = lax.dot_general(
                left, right, (((1,), (1,)), ((), ())), preferred_element_type=F32
            )
            product = jnp.where(keep, product, 0.0).reshape(2 * segments, BLOCK, lanes)
            diagonal[b] = jnp.sum(product, axis=1)

    for g in range(bins // LANES):
        for j in range(lanes // LANES):
            blocks = [diagonal[g * 8 + i, :, j * LANES : (j + 1) * LANES] for i in range(8)]
            for i, block in enumerate(exchange_lanes(blocks)):
                cross[j * 8 + i, :, g * LANES : (g + 1) * LANES] = block

    real, imag = cross[:, :segments, :], cross[:, segments:, :]
    cosine, sine = cos_ref[...][None], sin_ref[...][None]
    total = templates * segments
    delayed = jnp.concatenate(
        [
            (real * cosine + imag * sine).reshape(total, bins),
            (imag * cosine - real * sine).reshape(total, bins),
        ],
        axis=1,
    )
    delayed_high = delayed.astype(BF16)
    delayed_low = (delayed - delayed_high.astype(F32)).astype(BF16)
    tables_in[1].wait()
    both = jnp.dot(
        jnp.concatenate([delayed_high, delayed_low], axis=0), back[...], preferred_element_type=F32
    )
    result = both[:total] + both[total:]
    scores = result.reshape(templates, segments, length) * weights[...]
    stack = jnp.sum(scores, axis=1)
    for j in range(length // LANES):
        out_ref[j] = stack[:, j * LANES : (j + 1) * LANES]


def detect(pieces, lag_lengths, offsets, level, place, energy, forward, tmpl, back, cosine, sine, channel_total):
    segments, piece, channels = pieces[0].shape
    templates, length = lag_lengths.shape[0], energy.shape[1]
    bins = length // 2
    vmem = pl.BlockSpec(memory_space=pltpu.VMEM)
    smem = pl.BlockSpec(memory_space=pltpu.SMEM)
    anywhere = pl.BlockSpec(memory_space=pl.ANY)
    group = 8

    def kernel(*refs):
        detect_kernel(channel_total, *refs)

    return pl.pallas_call(
        kernel,
        in_specs=[vmem] * len(pieces) + [smem] * 4 + [vmem] + [anywhere] * 3 + [vmem] * 2,
        out_specs=vmem,
        out_shape=jax.ShapeDtypeStruct((length // LANES, templates, LANES), F32),
        scratch_shapes=[
            pltpu.VMEM(forward.shape, BF16),
            pltpu.VMEM(tmpl.shape, BF16),
            pltpu.VMEM(back.shape, BF16),
            pltpu.VMEM((templates, segments, length), F32),
            pltpu.VMEM((segments, 2 * length + LANES), F32),
            pltpu.VMEM((group, bins, channels), BF16),
            pltpu.VMEM((group, bins, channels), BF16),
            pltpu.VMEM((2, segments, bins, 2 * channels), BF16),
            pltpu.VMEM((bins // BLOCK, 2 * segments, templates * BLOCK), F32),
            pltpu.VMEM((templates, 2 * segments, bins), F32),
            pltpu.SemaphoreType.DMA((3,)),
        ],
        compiler_params=pltpu.CompilerParams(vmem_limit_bytes=44 << 20),
        cost_estimate=pl.CostEstimate(flops=12_000_000_000, bytes_accessed=24 << 20, transcendentals=0),
        name="detect",
    )(*pieces, lag_lengths, offsets, level, place, energy, forward, tmpl, back, cosine, sine)


def send(value, axis, move):
    return lax.ppermute(value, axis, [(i, move(i)) for i in range(lax.axis_size(axis))])


def apart(i):
    return (i + (-4 if i % 2 else 4)) % 16


def across(i):
    return i ^ 2


def sibling(i):
    return i ^ 1


def after(value, *earlier):
    return lax.optimization_barrier((value, *earlier))[0]


def body(samples, template_spectra, lag_lengths, offsets):
    segments, channels, piece = samples.shape
    chan_groups = lax.axis_size("chan")
    tmpl_groups = lax.axis_size("tmpl")
    channel_total = channels * chan_groups
    length = piece * tmpl_groups
    bins = length // 2
    templates = template_spectra.shape[1]
    me = lax.axis_index("tmpl")

    wide = samples.astype(F32)
    energy = jnp.sum(wide * wide, axis=1)

    def double(energy, bit, flip=0):
        other = send(energy, "tmpl", lambda i: i ^ bit ^ flip)
        upper = (me & bit) != 0
        return jnp.concatenate(
            [jnp.where(upper, other, energy), jnp.where(upper, energy, other)], axis=1
        )

    fence = lax.optimization_barrier
    own = jnp.transpose(samples, (0, 2, 1))
    beside_0 = send(own, "tmpl", apart)
    own_c = send(own, "tmpl", sibling)
    beside_1 = send(own_c, "tmpl", apart)
    energy = double(after(double(energy, 1), own_c), 2)
    own_x = send(own, "tmpl", across)
    energy_early = energy
    energy = double(energy, 4)
    far = send(beside_0, "tmpl", apart)
    tmpl, level = prepare_templates(after(template_spectra, energy_early))
    own_x, beside_1, level, energy = fence((own_x, beside_1, level, energy))

    far_x = send(far, "tmpl", across)
    energy = double(energy, 8, 4)
    own_xc = send(own_x, "tmpl", sibling)
    beside_0c, beside_1c = send(beside_0, "tmpl", sibling), send(beside_1, "tmpl", sibling)
    far_c = send(far, "tmpl", sibling)
    own_x, own_xc, energy = fence((own_x, own_xc, energy))
    beside_x0, beside_x1 = send(own_x, "tmpl", apart), send(own_xc, "tmpl", apart)
    sums = jnp.concatenate([energy, level], axis=1)
    sums = sums + send(sums, "chan", lambda i: i ^ 1)
    sums = sums + send(sums, "chan", lambda i: i ^ 3)
    sums = sums + send(sums, "chan", lambda i: i ^ 4)
    energy, level = sums[:, :length], sums[:, length]
    beside_x0c, beside_x1c = send(beside_x0, "tmpl", sibling), send(beside_x1, "tmpl", sibling)
    far_xc = send(far_x, "tmpl", sibling)

    order = bin_order(bins).astype(np.int32)
    phase = offsets[:, None] * order[None, :] % length
    angle = phase.astype(F32) * (2.0 * math.pi / length)
    cosine, sine = jnp.cos(angle), jnp.sin(angle)
    forward, back = tables(length)

    k = lax.iota(jnp.int32, 8)
    z = (me // 4 + jnp.where(k < 4, 0, 2 * (me % 2) - 1)) % 4
    start = (z % 2 * 4 + ((me ^ k) & 3)) * piece
    place = jnp.concatenate([start, jnp.where(z < 2, 1, -1)]).astype(jnp.int32)
    pieces = (
        own, own_c, own_x, own_xc, beside_0, beside_1, beside_x0, beside_x1,
        far, far_c, far_x, far_xc, beside_1c, beside_0c, beside_x1c, beside_x0c,
    )
    partial = detect(
        pieces, lag_lengths, offsets, level, place, energy, forward, tmpl, back, cosine, sine, channel_total
    )
    return jnp.sum(lax.all_to_all(partial, "chan", 0, 0, tiled=False), axis=0)


def solution(mesh):
    return jax.shard_map(
        body,
        mesh=mesh,
        in_specs=(P(None, "chan", "tmpl"), P(None, "tmpl", "chan", None), P("tmpl"), P()),
        out_specs=P("tmpl", "chan"),
        check_vma=False,
    )
```

```python
import math

import jax
import jax.numpy as jnp
import numpy as np
from jax import lax
from jax.experimental import pallas as pl
from jax.experimental.pallas import tpu as pltpu
from jax.sharding import PartitionSpec as P

epsilon = 1e-06
LANES = 128
BLOCK = 16
F32 = jnp.float32
BF16 = jnp.bfloat16


def bin_order(bins):
    return np.concatenate([np.arange(0, bins, 2), np.arange(1, bins, 2)])


def tables(length):
    bins = length // 2
    angle = 2.0 * np.pi * (np.outer(bin_order(bins), np.arange(length)) % length) / length
    cosine, sine = np.cos(angle), -np.sin(angle)
    near = bins // 2
    even = np.concatenate([cosine[:near, :bins], sine[:near, :bins]], axis=0)
    odd = np.concatenate([cosine[near:, :bins], sine[near:, :bins]], axis=0)
    backward = np.concatenate([cosine, sine], axis=0) * (2.0 / length)
    return np.stack([even, odd]).astype(BF16), backward.astype(BF16)


def turn(bins):
    return (np.arange(bins)[None, :] == bin_order(bins)[:, None]).astype(BF16)


def template_kernel(turn_ref, g_ref, out_ref, energy_ref):
    step, channels, bins = g_ref.shape[1:]
    block = turn_ref.shape[0]
    for t in range(step):
        total = jnp.zeros((8, bins), F32)
        for part in range(2):
            wide = g_ref[part, t].astype(F32)
            total = total + jnp.sum((wide * wide).reshape(channels // 8, 8, bins), axis=0)
            for j in range(bins // block):
                rows = lax.dot_general(
                    turn_ref[...], g_ref[part, t, :, j * block : (j + 1) * block],
                    (((1,), (1,)), ((), ())), preferred_element_type=F32,
                ).astype(BF16)
                half = block // 2 // BLOCK
                for parity in range(2):
                    first = parity * (bins // 2 // BLOCK) + j * half
                    out_ref[first : first + half, t, :, part * channels : (part + 1) * channels] = (
                        rows[parity * block // 2 : (parity + 1) * block // 2].reshape(half, BLOCK, channels)
                    )
        level = jnp.sum(jnp.sum(total, axis=0, keepdims=True), axis=1, keepdims=True) * (1.0 / bins)
        energy_ref[pl.ds(pl.program_id(0) * step + t, 1), :] = jnp.broadcast_to(level, (1, LANES))


def prepare_templates(template_spectra):
    _, templates, channels, bins = template_spectra.shape
    step = 4
    matrix = turn(256)
    return pl.pallas_call(
        template_kernel,
        grid=(templates // step,),
        in_specs=[
            pl.BlockSpec(matrix.shape, lambda t: (0, 0)),
            pl.BlockSpec((2, step, channels, bins), lambda t: (0, t, 0, 0)),
        ],
        out_specs=[
            pl.BlockSpec((bins // BLOCK, step, BLOCK, 2 * channels), lambda t: (0, t, 0, 0)),
            pl.BlockSpec((templates, LANES), lambda t: (0, 0)),
        ],
        out_shape=[
            jax.ShapeDtypeStruct((bins // BLOCK, templates, BLOCK, 2 * channels), BF16),
            jax.ShapeDtypeStruct((templates, LANES), F32),
        ],
        compiler_params=pltpu.CompilerParams(vmem_limit_bytes=56 << 20),
        cost_estimate=pl.CostEstimate(flops=2_200_000_000, bytes_accessed=16 << 20, transcendentals=0),
        name="template_flip",
    )(matrix, template_spectra)


def weight_kernel(channel_total, scale, lag_ref, offset_ref, level_ref, energy_ref, out_ref, prefix):
    segments, length = energy_ref.shape
    templates = out_ref.shape[0]
    row = lax.broadcasted_iota(jnp.int32, (segments, length), 0)
    energy = energy_ref[...]
    delayed = jnp.zeros((segments, length), F32)
    for s in range(segments):
        delayed = jnp.where(row == s, pltpu.roll(energy, offset_ref[s], axis=1), delayed)
    before = lax.broadcasted_iota(jnp.int32, (LANES, LANES), 0) < lax.broadcasted_iota(
        jnp.int32, (LANES, LANES), 1
    )
    before = before.astype(F32)
    carry = jnp.zeros((segments, 1), F32)
    blocks = length // LANES
    for j in range(blocks):
        piece = delayed[:, j * LANES : (j + 1) * LANES]
        prefix[:, j * LANES : (j + 1) * LANES] = carry + jnp.dot(
            piece, before, precision=lax.Precision.HIGHEST, preferred_element_type=F32
        )
        carry = carry + jnp.sum(piece, axis=1, keepdims=True)
    first = prefix[:, :length]
    prefix[:, length : 2 * length] = first + carry
    prefix[:, 2 * length :] = first[:, :LANES] + 2.0 * carry
    span = length + LANES
    for t in range(templates):
        lag = lag_ref[t]
        start = pl.multiple_of((lag // LANES) * LANES, LANES)
        ahead = pltpu.roll(prefix[:, pl.ds(start, span)], span - lag % LANES, axis=1)[:, :length]
        power = (ahead - first) / (channel_total * lag.astype(F32))
        out_ref[t] = scale * lax.rsqrt(level_ref[t] * power + epsilon)


def store_spectra(spectra, s, forward, summed, differed):
    near, channels = forward.shape[1] // 2, summed.shape[-1]
    for parity, record in enumerate((summed, differed)):
        first = parity * near
        result = jnp.dot(forward[parity], record[...], preferred_element_type=F32).astype(BF16)
        real, imag = result[:near], result[near:]
        spectra[0, s, first : first + near, :channels] = real
        spectra[0, s, first : first + near, channels:] = imag
        spectra[1, s, first : first + near, :channels] = imag
        spectra[1, s, first : first + near, channels:] = -real


def exchange_lanes(blocks):
    blocks = list(blocks)
    index = lax.broadcasted_iota(jnp.int32, blocks[0].shape, 1) // BLOCK
    for bit in (1, 2, 4):
        upper = (index & bit) != 0
        for i in range(8):
            if i & bit:
                continue
            first, second = blocks[i], blocks[i + bit]
            shift = BLOCK * bit
            blocks[i] = jnp.where(upper, pltpu.roll(second, shift, axis=1), first)
            blocks[i + bit] = jnp.where(upper, second, pltpu.roll(first, LANES - shift, axis=1))
    return blocks


def detect_kernel(channel_total, *refs):
    sources, refs = refs[:16], refs[16:]
    lag_ref, offset_ref, level_ref, place_ref, energy_ref = refs[:5]
    forward_hbm, tmpl_hbm, back_hbm, cos_ref, sin_ref, out_ref = refs[5:11]
    forward, tmpl, back, weights, prefix, summed, differed, spectra, diagonal, cross, sems = refs[11:]
    segments, piece, channels = sources[0].shape
    templates, _, length = weights.shape
    bins = length // 2
    lanes = templates * BLOCK
    group = summed.shape[0]
    tables_in = [
        pltpu.make_async_copy(source, target, sems.at[j])
        for j, (source, target) in enumerate(
            ((forward_hbm, forward), (back_hbm, back))
        )
    ]
    copy_tmpl = pltpu.make_async_copy(tmpl_hbm, tmpl, sems.at[2])
    for copy in (tables_in[0], copy_tmpl, tables_in[1]):
        copy.start()
    weight_kernel(channel_total, 1.0 / math.sqrt(segments), lag_ref, offset_ref, level_ref, energy_ref, weights, prefix)

    pairs = len(sources) // 2
    starts = [pl.multiple_of(place_ref[k], piece) for k in range(pairs)]
    signs = [place_ref[pairs + k].astype(F32).astype(BF16) for k in range(pairs)]
    tables_in[0].wait()

    @pl.loop(0, segments // group)
    def _(i):
        for u in range(group):
            s = i * group + u
            for k in range(pairs):
                first, second = sources[k][s], sources[pairs + k][s]
                summed[u, pl.ds(starts[k], piece), :] = first + second
                differed[u, pl.ds(starts[k], piece), :] = (first - second) * signs[k]
            store_spectra(spectra, s, forward, summed.at[u], differed.at[u])

    copy_tmpl.wait()
    rows = 2 * segments * BLOCK
    keep = (
        lax.broadcasted_iota(jnp.int32, (rows, lanes), 0) % BLOCK
        == lax.broadcasted_iota(jnp.int32, (rows, lanes), 1) % BLOCK
    )

    @pl.loop(0, bins // BLOCK // 32)
    def _(i):
        for u in range(32):
            b = i * 32 + u
            start = pl.multiple_of(b * BLOCK, BLOCK)
            left = spectra[:, :, pl.ds(start, BLOCK), :].reshape(rows, 2 * channels)
            right = tmpl[b].reshape(lanes, 2 * channels)
            product = lax.dot_general(
                left, right, (((1,), (1,)), ((), ())), preferred_element_type=F32
            )
            product = jnp.where(keep, product, 0.0).reshape(2 * segments, BLOCK, lanes)
            diagonal[b] = jnp.sum(product, axis=1)

    for g in range(bins // LANES):
        for j in range(lanes // LANES):
            blocks = [diagonal[g * 8 + i, :, j * LANES : (j + 1) * LANES] for i in range(8)]
            for i, block in enumerate(exchange_lanes(blocks)):
                cross[j * 8 + i, :, g * LANES : (g + 1) * LANES] = block

    real, imag = cross[:, :segments, :], cross[:, segments:, :]
    cosine, sine = cos_ref[...][None], sin_ref[...][None]
    total = templates * segments
    delayed = jnp.concatenate(
        [
            (real * cosine + imag * sine).reshape(total, bins),
            (imag * cosine - real * sine).reshape(total, bins),
        ],
        axis=1,
    )
    delayed_high = delayed.astype(BF16)
    delayed_low = (delayed - delayed_high.astype(F32)).astype(BF16)
    tables_in[1].wait()
    both = jnp.dot(
        jnp.concatenate([delayed_high, delayed_low], axis=0), back[...], preferred_element_type=F32
    )
    result = both[:total] + both[total:]
    scores = result.reshape(templates, segments, length) * weights[...]
    stack = jnp.sum(scores, axis=1)
    for j in range(length // LANES):
        out_ref[j] = stack[:, j * LANES : (j + 1) * LANES]


def detect(pieces, lag_lengths, offsets, level, place, energy, forward, tmpl, back, cosine, sine, channel_total):
    segments, piece, channels = pieces[0].shape
    templates, length = lag_lengths.shape[0], energy.shape[1]
    bins = length // 2
    vmem = pl.BlockSpec(memory_space=pltpu.VMEM)
    smem = pl.BlockSpec(memory_space=pltpu.SMEM)
    anywhere = pl.BlockSpec(memory_space=pl.ANY)
    group = 8

    def kernel(*refs):
        detect_kernel(channel_total, *refs)

    return pl.pallas_call(
        kernel,
        in_specs=[vmem] * len(pieces) + [smem] * 4 + [vmem] + [anywhere] * 3 + [vmem] * 2,
        out_specs=vmem,
        out_shape=jax.ShapeDtypeStruct((length // LANES, templates, LANES), F32),
        scratch_shapes=[
            pltpu.VMEM(forward.shape, BF16),
            pltpu.VMEM(tmpl.shape, BF16),
            pltpu.VMEM(back.shape, BF16),
            pltpu.VMEM((templates, segments, length), F32),
            pltpu.VMEM((segments, 2 * length + LANES), F32),
            pltpu.VMEM((group, bins, channels), BF16),
            pltpu.VMEM((group, bins, channels), BF16),
            pltpu.VMEM((2, segments, bins, 2 * channels), BF16),
            pltpu.VMEM((bins // BLOCK, 2 * segments, templates * BLOCK), F32),
            pltpu.VMEM((templates, 2 * segments, bins), F32),
            pltpu.SemaphoreType.DMA((3,)),
        ],
        compiler_params=pltpu.CompilerParams(vmem_limit_bytes=44 << 20),
        cost_estimate=pl.CostEstimate(flops=12_000_000_000, bytes_accessed=24 << 20, transcendentals=0),
        name="detect",
    )(*pieces, lag_lengths, offsets, level, place, energy, forward, tmpl, back, cosine, sine)


def send(value, axis, move):
    return lax.ppermute(value, axis, [(i, move(i)) for i in range(lax.axis_size(axis))])


def apart(i):
    return (i + (-4 if i % 2 else 4)) % 16


def across(i):
    return i ^ 2


def sibling(i):
    return i ^ 1


def after(value, *earlier):
    return lax.optimization_barrier((value, *earlier))[0]


def body(samples, template_spectra, lag_lengths, offsets):
    segments, channels, piece = samples.shape
    chan_groups = lax.axis_size("chan")
    tmpl_groups = lax.axis_size("tmpl")
    channel_total = channels * chan_groups
    length = piece * tmpl_groups
    bins = length // 2
    templates = template_spectra.shape[1]
    me = lax.axis_index("tmpl")

    wide = samples.astype(F32)
    energy = jnp.sum(wide * wide, axis=1)

    def double(energy, bit, flip=0):
        other = send(energy, "tmpl", lambda i: i ^ bit ^ flip)
        upper = (me & bit) != 0
        return jnp.concatenate(
            [jnp.where(upper, other, energy), jnp.where(upper, energy, other)], axis=1
        )

    fence = lax.optimization_barrier
    own = jnp.transpose(samples, (0, 2, 1))
    beside_0 = send(own, "tmpl", apart)
    own_c = send(own, "tmpl", sibling)
    beside_1 = send(own_c, "tmpl", apart)
    energy = double(after(double(energy, 1), own_c), 2)
    own_x = send(own, "tmpl", across)
    energy_early = energy
    energy = double(energy, 4)
    far = send(beside_0, "tmpl", apart)
    tmpl, level = prepare_templates(after(template_spectra, energy_early))
    own_x, beside_1, level, energy = fence((own_x, beside_1, level, energy))

    far_x = send(far, "tmpl", across)
    energy = double(energy, 8, 4)
    own_xc = send(own_x, "tmpl", sibling)
    beside_0c, beside_1c = send(beside_0, "tmpl", sibling), send(beside_1, "tmpl", sibling)
    far_c = send(far, "tmpl", sibling)
    own_x, own_xc, energy = fence((own_x, own_xc, energy))
    beside_x0, beside_x1 = send(own_x, "tmpl", apart), send(own_xc, "tmpl", apart)
    sums = jnp.concatenate([energy, level], axis=1)
    sums = sums + send(sums, "chan", lambda i: i ^ 1)
    sums = sums + send(sums, "chan", lambda i: i ^ 3)
    sums = sums + send(sums, "chan", lambda i: i ^ 4)
    energy, level = sums[:, :length], sums[:, length]
    beside_x0c, beside_x1c = send(beside_x0, "tmpl", sibling), send(beside_x1, "tmpl", sibling)
    far_xc = send(far_x, "tmpl", sibling)

    order = bin_order(bins).astype(np.int32)
    phase = offsets[:, None] * order[None, :] % length
    angle = phase.astype(F32) * (2.0 * math.pi / length)
    cosine, sine = jnp.cos(angle), jnp.sin(angle)
    forward, back = tables(length)

    k = lax.iota(jnp.int32, 8)
    z = (me // 4 + jnp.where(k < 4, 0, 2 * (me % 2) - 1)) % 4
    start = (z % 2 * 4 + ((me ^ k) & 3)) * piece
    place = jnp.concatenate([start, jnp.where(z < 2, 1, -1)]).astype(jnp.int32)
    pieces = (
        own, own_c, own_x, own_xc, beside_0, beside_1, beside_x0, beside_x1,
        far, far_c, far_x, far_xc, beside_1c, beside_0c, beside_x1c, beside_x0c,
    )
    partial = detect(
        pieces, lag_lengths, offsets, level, place, energy, forward, tmpl, back, cosine, sine, channel_total
    )
    return jnp.sum(lax.all_to_all(partial, "chan", 0, 0, tiled=False), axis=0)


def solution(mesh):
    return jax.shard_map(
        body,
        mesh=mesh,
        in_specs=(P(None, "chan", "tmpl"), P(None, "tmpl", "chan", None), P("tmpl"), P()),
        out_specs=P("tmpl", "chan"),
        check_vma=False,
    )
```
